1024 devices in a mesh: leaf: 64 (over z, x_hi), panel: 16 (over y, x_lo, core).
Axes of the slice: x: 4 (x_hi: 2, x_lo: 2; x = x_hi * 2 + x_lo), y: 4, z: 32, core: 2. Of those that a mesh axis runs over, the one named last changes fastest.
Arguments:
- coupling: bfloat16 [64, 4096, 2048], P('leaf', 'panel'), may hold values from -6 to 6
- modes: bfloat16 [64, 2048, 256], P('leaf'), may hold values from -0.125 to 0.125
- eigvals: float32 [64, 256], P('leaf'), may hold values from 16 to 256
- sep_stiffness: bfloat16 [64, 4096, 2048], P('leaf', 'panel'), may hold values from -6 to 6
Outputs:
- reduced: bfloat16 [64, 4096, 2048], P('leaf', 'panel')
The draws below stay inside these ranges and needn't reach their ends.
All inputs are finite; a program needn't handle non-finite values.
Results may differ from the reference program's by a relative error of at most 0.0042.
Values may be sent and summed in bfloat16 or wider, within the bound.
No kernel may reach another device: no remote copies, remote signals or barrier semaphores. Data moves between devices by JAX's collectives and lax.ppermute only.
A program may use at most 32 MiB of HBM per device.

```python
import math
import jax
import jax.numpy as jnp
from jax import lax

SEP = 4096
MODES = 256
BND = 2048
LEAVES = 64


def block_scale(key, dims, pieces, least, largest):
    def one(axis_at, blocks):
        heights = jax.random.uniform(jax.random.fold_in(jax.random.fold_in(key, 6), axis_at), (blocks,), jnp.float32, least / len(pieces), largest / len(pieces))
        return jnp.repeat(jnp.exp(heights), dims[axis_at] // blocks).reshape((-1,) + (1,) * (len(dims) - axis_at - 1))

    gain = one(*pieces[0])
    for cut in pieces[1:]:
        gain = gain * one(*cut)
    return gain


def normal_values(own_key, shape, scale, bound, shards=(), kind=jnp.bfloat16):
    values = jax.random.normal(own_key, shape, jnp.float32) * scale
    if len(shards) > 0:
        values = block_scale(own_key, shape, shards, -0.22, 0.18) * values
    return jnp.clip(values, min=-bound, max=bound).astype(kind)


def setup_inputs(seed: int = 0) -> dict:
    splits = jax.random.split(jax.random.key(seed), 5)
    coupling = normal_values(splits[0], (LEAVES, SEP, BND), 1.0, 6.0, ((0, 64), (1, 16)))
    modes = normal_values(splits[1], (LEAVES, BND, MODES), BND ** -0.5, 0.125, ((0, 64),))
    eigvals = jnp.clip(jnp.exp(math.log(256.0) - 2.7725887 * jax.random.uniform(splits[2], (LEAVES, MODES), jnp.float32) ** block_scale(splits[2], (LEAVES, MODES), ((0, 64),), -0.2, 0.2)), 16.0, 256.0)
    sep_stiffness = normal_values(splits[3], (LEAVES, SEP, SEP // 2), 1.0, 6.0, ((0, 64), (1, 16)))
    return {"coupling": coupling, "modes": modes, "eigvals": eigvals, "sep_stiffness": sep_stiffness}


def reduce_parent(items):
    coupling_pair, modes_pair, eig_pair, stiff_pair = items
    scaled_list = []
    for child in range(2):
        projected = jnp.dot(coupling_pair[child], modes_pair[child], preferred_element_type=jnp.float32)
        scaled_list.append((projected * lax.rsqrt(eig_pair[child])[None, :]).astype(jnp.bfloat16))
    joined = jnp.concatenate(scaled_list, axis=1)
    congruence = jnp.dot(joined, joined.T, preferred_element_type=jnp.float32)
    half_cols = SEP // 2
    first = stiff_pair[0].astype(jnp.float32) - congruence[:, :half_cols]
    second = stiff_pair[1].astype(jnp.float32) - congruence[:, half_cols:]
    return jnp.stack([first, second]).astype(jnp.bfloat16)

def reference(coupling, modes, eigvals, sep_stiffness):
    parents = LEAVES // 2
    items = (coupling.reshape(parents, 2, SEP, BND), modes.reshape(parents, 2, BND, MODES), eigvals.reshape(parents, 2, MODES), sep_stiffness.reshape(parents, 2, SEP, SEP // 2))
    result = lax.map(reduce_parent, items)
    return result.reshape(LEAVES, SEP, SEP // 2)
```

```python
import functools

import jax
import jax.numpy as jnp
from jax import lax
from jax.experimental import pallas as pl
from jax.experimental.pallas import tpu as pltpu
from jax.sharding import PartitionSpec as P

AXES = ("leaf", "panel")
PANELS = 16
VMEM = pl.BlockSpec(memory_space=pltpu.VMEM)
HBM = pl.BlockSpec(memory_space=pltpu.HBM)


def pairs(move):
    found = []
    for parent in range(lax.axis_size("leaf") // 2):
        for bit in range(2):
            for panel in range(PANELS):
                target = move(bit, panel)
                if target is not None:
                    found.append((
                        (2 * parent + bit) * PANELS + panel,
                        (2 * parent + target[0]) * PANELS + target[1],
                    ))
    return found


def to_sibling(bit, panel):
    return (1 - bit, panel)


def to_far_rows(bit, panel):
    return (bit, panel ^ 12) if panel // 8 == bit else None


def to_core(bit, panel):
    return (bit, panel ^ 1)


def project_kernel(parts, coupling, modes, eigvals, scaled, a, b, sems):
    depth = a.shape[1] // parts
    copies = []
    for k in range(parts):
        cut = pl.ds(k * depth, depth)
        copies.append((
            pltpu.make_async_copy(coupling.at[0, :, cut], a.at[:, cut], sems.at[0, k]),
            pltpu.make_async_copy(modes.at[0, cut, :], b.at[cut, :], sems.at[1, k]),
        ))
    for pair in copies:
        for copy in pair:
            copy.start()
    total = jnp.zeros(scaled.shape, jnp.float32)
    for k, pair in enumerate(copies):
        for copy in pair:
            copy.wait()
        total += jnp.dot(
            a[:, k * depth : (k + 1) * depth],
            b[k * depth : (k + 1) * depth, :],
            preferred_element_type=jnp.float32,
        )
    scaled[...] = (total * lax.rsqrt(eigvals[...])).astype(jnp.bfloat16)


def project(coupling, modes, eigvals):
    rows, depth, columns = coupling.shape[1], coupling.shape[2], modes.shape[2]
    parts = 4
    return pl.pallas_call(
        functools.partial(project_kernel, parts),
        out_shape=jax.ShapeDtypeStruct((rows, columns), jnp.bfloat16),
        in_specs=[HBM, HBM, VMEM],
        out_specs=VMEM,
        scratch_shapes=[
            pltpu.VMEM((rows, depth), jnp.bfloat16),
            pltpu.VMEM((depth, columns), jnp.bfloat16),
            pltpu.SemaphoreType.DMA((2, parts)),
        ],
        compiler_params=pltpu.CompilerParams(vmem_limit_bytes=60 * 2**20),
        name="project",
    )(coupling, modes, eigvals)


def update_kernel(other_core, own, sibling, pieces, stiffness, so_far, out, held, made, in_sems, out_sems):
    del so_far
    bit = lax.axis_index("leaf") % 2
    core = lax.axis_index("panel") % 2
    core = 1 - core if other_core else core
    width = own.shape[0]
    loads, stores = [], []
    for n in range(4):
        cut = pl.ds(pl.multiple_of((2 * n + core) * width, width), width)
        loads.append(pltpu.make_async_copy(stiffness.at[0, :, cut], held.at[n], in_sems.at[n]))
        stores.append(pltpu.make_async_copy(made.at[n], out.at[0, :, cut], out_sems.at[n]))
    for copy in loads:
        copy.start()
    for n in range(4):
        ours = pieces[(1 - bit) * 4 + (n ^ 2)]
        others = pieces[bit * 4 + n]
        block = lax.dot_general(
            own[...], ours, (((1,), (1,)), ((), ())), preferred_element_type=jnp.float32
        ) + lax.dot_general(
            sibling[...], others, (((1,), (1,)), ((), ())), preferred_element_type=jnp.float32
        )
        loads[n].wait()
        made[n] = (held[n].astype(jnp.float32) - block).astype(jnp.bfloat16)
        stores[n].start()
    for copy in stores:
        copy.wait()


def update(other_core, own, sibling, pieces, stiffness, so_far):
    rows = own.shape[0]
    first = so_far is None
    kernel = functools.partial(update_kernel, other_core)
    if first:
        kernel = lambda own, sibling, pieces, stiffness, *rest: update_kernel(
            other_core, own, sibling, pieces, stiffness, None, *rest
        )
    return pl.pallas_call(
        kernel,
        out_shape=jax.ShapeDtypeStruct(stiffness.shape, stiffness.dtype),
        in_specs=[VMEM, VMEM, VMEM, HBM] + ([] if first else [HBM]),
        out_specs=HBM,
        scratch_shapes=[
            pltpu.VMEM((4, rows, rows), jnp.bfloat16),
            pltpu.VMEM((4, rows, rows), jnp.bfloat16),
            pltpu.SemaphoreType.DMA((4,)),
            pltpu.SemaphoreType.DMA((4,)),
        ],
        input_output_aliases={} if first else {4: 0},
        compiler_params=pltpu.CompilerParams(vmem_limit_bytes=16 * 2**20),
        cost_estimate=pl.CostEstimate(
            flops=2 * rows * 2 * rows * 4 * rows, bytes_accessed=6 * 2**20, transcendentals=0
        ),
        name="update_other" if other_core else "update_own",
    )(own, sibling, pieces, stiffness, *([] if first else [so_far]))


def shards(coupling, modes, eigvals, sep_stiffness):
    scaled = project(coupling, modes, eigvals)
    bit = lax.axis_index("leaf") % 2
    here = lax.axis_index("panel") // 8 == bit

    sibling = lax.ppermute(scaled, AXES, pairs(to_sibling))
    handed = lax.ppermute(scaled, AXES, pairs(to_far_rows))
    held = jnp.where(here, sibling, handed)
    groups = [list(range(core, PANELS, 2)) for core in range(2)]
    sent = jnp.broadcast_to(held[None], (8,) + held.shape)
    mine = lax.all_to_all(sent, "panel", 0, 0, axis_index_groups=groups)
    theirs = lax.ppermute(mine, AXES, pairs(to_core))
    half = update(False, scaled, sibling, mine, sep_stiffness, None)
    return update(True, scaled, sibling, theirs, sep_stiffness, half)


def solution(mesh):
    placed = (
        P("leaf", "panel", None),
        P("leaf", None, None),
        P("leaf", None),
        P("leaf", "panel", None),
    )
    return jax.shard_map(
        shards, mesh=mesh, in_specs=placed, out_specs=P("leaf", "panel", None), check_vma=False
    )
```

```python
import functools

import jax
import jax.numpy as jnp
from jax import lax
from jax.experimental import pallas as pl
from jax.experimental.pallas import tpu as pltpu
from jax.sharding import PartitionSpec as P

AXES = ("leaf", "panel")
PANELS = 16
VMEM = pl.BlockSpec(memory_space=pltpu.VMEM)
HBM = pl.BlockSpec(memory_space=pltpu.HBM)


def pairs(move):
    found = []
    for parent in range(lax.axis_size("leaf") // 2):
        for bit in range(2):
            for panel in range(PANELS):
                target = move(bit, panel)
                if target is not None:
                    found.append((
                        (2 * parent + bit) * PANELS + panel,
                        (2 * parent + target[0]) * PANELS + target[1],
                    ))
    return found


def across(bit, panel):
    return None if panel // 8 == bit else (1 - bit, panel ^ 14)


def to_sibling(bit, panel):
    return (1 - bit, panel) if panel // 8 == bit else None


def to_core(bit, panel):
    return (bit, panel ^ 1)


def project_kernel(parts, coupling, modes, eigvals, scaled, a, b, e, sems, last):
    depth = a.shape[1] // parts
    copies = []
    for k in range(parts):
        cut = pl.ds(k * depth, depth)
        copies.append((
            pltpu.make_async_copy(coupling.at[0, :, cut], a.at[:, cut], sems.at[0, k]),
            pltpu.make_async_copy(modes.at[0, cut, :], b.at[cut, :], sems.at[1, k]),
        ))
    for pair in copies:
        for copy in pair:
            copy.start()
    gains = pltpu.make_async_copy(eigvals, e, last)
    gains.start()
    total = jnp.zeros(scaled.shape, jnp.float32)
    for k, pair in enumerate(copies):
        for copy in pair:
            copy.wait()
        total += jnp.dot(
            a[:, k * depth : (k + 1) * depth],
            b[k * depth : (k + 1) * depth, :],
            preferred_element_type=jnp.float32,
        )
    gains.wait()
    scaled[...] = (total * lax.rsqrt(e[...])).astype(jnp.bfloat16)


def project(coupling, modes, eigvals):
    rows, depth, columns = coupling.shape[1], coupling.shape[2], modes.shape[2]
    parts = 4
    return pl.pallas_call(
        functools.partial(project_kernel, parts),
        out_shape=jax.ShapeDtypeStruct((rows, columns), jnp.bfloat16),
        in_specs=[HBM, HBM, HBM],
        out_specs=VMEM,
        scratch_shapes=[
            pltpu.VMEM((rows, depth), jnp.bfloat16),
            pltpu.VMEM((depth, columns), jnp.bfloat16),
            pltpu.VMEM((1, columns), jnp.float32),
            pltpu.SemaphoreType.DMA((2, parts)),
            pltpu.SemaphoreType.DMA,
        ],
        compiler_params=pltpu.CompilerParams(vmem_limit_bytes=53 * 2**20),
        name="project",
    )(coupling, modes, eigvals)


def update_kernel(other_core, own, sibling, mine, pieces, stiffness, out, made, sems):
    bit, panel = lax.axis_index("leaf") % 2, lax.axis_index("panel")
    core = 1 - panel % 2 if other_core else panel % 2
    here = panel // 8 == bit
    width = own.shape[0]
    partner = jnp.where(here, mine[(1 - bit) * 4 + 3 - (panel % 8) // 2], sibling[...])
    stores = []
    for n in range(4):
        cut = pl.ds(pl.multiple_of((2 * n + core) * width, width), width)
        block = lax.dot_general(
            own[...], pieces[bit * 4 + n], (((1,), (1,)), ((), ())), preferred_element_type=jnp.float32
        ) + lax.dot_general(
            partner,
            pieces[(1 - bit) * 4 + 3 - n],
            (((1,), (1,)), ((), ())),
            preferred_element_type=jnp.float32,
        )
        made[n] = (stiffness[0, :, cut].astype(jnp.float32) - block).astype(jnp.bfloat16)
        stores.append(pltpu.make_async_copy(made.at[n], out.at[0, :, cut], sems.at[n]))
        stores[n].start()
    for copy in stores:
        copy.wait()


def update_own_kernel(own, sibling, mine, stiffness, *rest):
    update_kernel(False, own, sibling, mine, mine, stiffness, *rest)


def update_other_kernel(own, sibling, mine, theirs, stiffness, so_far, *rest):
    del so_far
    update_kernel(True, own, sibling, mine, theirs, stiffness, *rest)


def update(kernel, name, arrays, stiffness, so_far):
    rows = arrays[0].shape[0]
    before = [] if so_far is None else [so_far]
    count = len(arrays) + 1
    return pl.pallas_call(
        kernel,
        out_shape=jax.ShapeDtypeStruct(stiffness.shape, stiffness.dtype),
        in_specs=[VMEM] * count + [HBM] * len(before),
        out_specs=HBM,
        scratch_shapes=[
            pltpu.VMEM((4, rows, rows), jnp.bfloat16),
            pltpu.SemaphoreType.DMA((4,)),
        ],
        input_output_aliases={count: 0} if before else {},
        compiler_params=pltpu.CompilerParams(vmem_limit_bytes=16 * 2**20),
        cost_estimate=pl.CostEstimate(
            flops=2 * rows * 2 * rows * 4 * rows, bytes_accessed=2 * 2**20, transcendentals=0
        ),
        name=name,
    )(*arrays, stiffness, *before)


def shards(coupling, modes, eigvals, sep_stiffness):
    scaled = project(coupling, modes, eigvals)
    bit = lax.axis_index("leaf") % 2
    here = lax.axis_index("panel") // 8 == bit

    crossed = lax.ppermute(scaled, AXES, pairs(across))
    sibling = lax.ppermute(scaled, AXES, pairs(to_sibling))
    held = jnp.where(here, scaled, crossed)
    held, sibling = lax.optimization_barrier((held, sibling))
    groups = [list(range(core, PANELS, 2)) for core in range(2)]
    sent = jnp.broadcast_to(held[None], (8,) + held.shape)
    mine = lax.all_to_all(sent, "panel", 0, 0, axis_index_groups=groups)
    theirs = lax.ppermute(mine, AXES, pairs(to_core))
    half = update(update_own_kernel, "update_own", (scaled, sibling, mine), sep_stiffness, None)
    return update(update_other_kernel, "update_other", (scaled, sibling, mine, theirs), sep_stiffness, half)


def solution(mesh):
    placed = (
        P("leaf", "panel", None),
        P("leaf", None, None),
        P("leaf", None),
        P("leaf", "panel", None),
    )
    return jax.shard_map(
        shards, mesh=mesh, in_specs=placed, out_specs=P("leaf", "panel", None), check_vma=False
    )
```

```python
import functools

import jax
import jax.numpy as jnp
from jax import lax
from jax.experimental import pallas as pl
from jax.experimental.pallas import tpu as pltpu
from jax.sharding import PartitionSpec as P

AXES = ("leaf", "panel")
PANELS = 16
PROJECT_VMEM = 211 * 2**18
VMEM = pl.BlockSpec(memory_space=pltpu.VMEM)
HBM = pl.BlockSpec(memory_space=pltpu.HBM)


def pairs(move):
    found = []
    for parent in range(lax.axis_size("leaf") // 2):
        for bit in range(2):
            for panel in range(PANELS):
                target = move(bit, panel)
                if target is not None:
                    found.append((
                        (2 * parent + bit) * PANELS + panel,
                        (2 * parent + target[0]) * PANELS + target[1],
                    ))
    return found


def across(bit, panel):
    return None if panel // 8 == bit else (1 - bit, panel ^ 14)


def to_sibling(bit, panel):
    return (1 - bit, panel) if panel // 8 == bit else None


def to_core(bit, panel):
    return (bit, panel ^ 1)


def project_kernel(parts, coupling, modes, projected, a, b, sems):
    depth = a.shape[1] // parts
    copies = []
    for k in range(parts):
        cut = pl.ds(k * depth, depth)
        copies.append((
            pltpu.make_async_copy(coupling.at[0, :, cut], a.at[:, cut], sems.at[0, k]),
            pltpu.make_async_copy(modes.at[0, cut, :], b.at[cut, :], sems.at[1, k]),
        ))
    for pair in copies:
        for copy in pair:
            copy.start()
    total = None
    for k, pair in enumerate(copies):
        for copy in pair:
            copy.wait()
        term = jnp.dot(
            a[:, k * depth : (k + 1) * depth],
            b[k * depth : (k + 1) * depth, :],
            preferred_element_type=jnp.float32,
        )
        total = term if total is None else total + term
    projected[...] = total


def project(coupling, modes):
    rows, depth, columns = coupling.shape[1], coupling.shape[2], modes.shape[2]
    parts = 2
    return pl.pallas_call(
        functools.partial(project_kernel, parts),
        out_shape=jax.ShapeDtypeStruct((rows, columns), jnp.float32),
        in_specs=[HBM, HBM],
        out_specs=VMEM,
        scratch_shapes=[
            pltpu.VMEM((rows, depth), jnp.bfloat16),
            pltpu.VMEM((depth, columns), jnp.bfloat16),
            pltpu.SemaphoreType.DMA((2, parts)),
        ],
        compiler_params=pltpu.CompilerParams(vmem_limit_bytes=PROJECT_VMEM),
        name="project",
    )(coupling, modes)


def update_kernel(other_core, own, sibling, mine, pieces, stiffness, out, made, sems):
    bit, panel = lax.axis_index("leaf") % 2, lax.axis_index("panel")
    core = 1 - panel % 2 if other_core else panel % 2
    here = panel // 8 == bit
    width = own.shape[0]
    partner = jnp.where(here, mine[(1 - bit) * 4 + 3 - (panel % 8) // 2], sibling[...])
    stores = []
    for n in range(4):
        cut = pl.ds(pl.multiple_of((2 * n + core) * width, width), width)
        block = lax.dot_general(
            own[...], pieces[bit * 4 + n], (((1,), (1,)), ((), ())), preferred_element_type=jnp.float32
        ) + lax.dot_general(
            partner,
            pieces[(1 - bit) * 4 + 3 - n],
            (((1,), (1,)), ((), ())),
            preferred_element_type=jnp.float32,
        )
        made[n] = (stiffness[0, :, cut].astype(jnp.float32) - block).astype(jnp.bfloat16)
        stores.append(pltpu.make_async_copy(made.at[n], out.at[0, :, cut], sems.at[n]))
        stores[n].start()
    for copy in stores:
        copy.wait()


def update_own_kernel(own, sibling, mine, stiffness, *rest):
    update_kernel(False, own, sibling, mine, mine, stiffness, *rest)


def update_other_kernel(own, sibling, mine, theirs, stiffness, so_far, *rest):
    del so_far
    update_kernel(True, own, sibling, mine, theirs, stiffness, *rest)


def update(kernel, name, arrays, stiffness, so_far):
    rows = arrays[0].shape[0]
    before = [] if so_far is None else [so_far]
    count = len(arrays) + 1
    return pl.pallas_call(
        kernel,
        out_shape=jax.ShapeDtypeStruct(stiffness.shape, stiffness.dtype),
        in_specs=[VMEM] * count + [HBM] * len(before),
        out_specs=HBM,
        scratch_shapes=[
            pltpu.VMEM((4, rows, rows), jnp.bfloat16),
            pltpu.SemaphoreType.DMA((4,)),
        ],
        input_output_aliases={count: 0} if before else {},
        compiler_params=pltpu.CompilerParams(vmem_limit_bytes=16 * 2**20),
        cost_estimate=pl.CostEstimate(
            flops=2 * rows * 2 * rows * 4 * rows, bytes_accessed=2 * 2**20, transcendentals=0
        ),
        name=name,
    )(*arrays, stiffness, *before)


def shards(coupling, modes, eigvals, sep_stiffness):
    projected, eigvals = lax.optimization_barrier((project(coupling, modes), eigvals))
    scaled = (projected * lax.rsqrt(eigvals[0])[None, :]).astype(jnp.bfloat16)
    bit = lax.axis_index("leaf") % 2
    here = lax.axis_index("panel") // 8 == bit

    sibling = lax.ppermute(scaled, AXES, pairs(to_sibling))
    crossed = lax.ppermute(scaled, AXES, pairs(across))
    crossed, sibling = lax.optimization_barrier((crossed, sibling))
    held = jnp.where(here, scaled, crossed)
    groups = [list(range(core, PANELS, 2)) for core in range(2)]
    sent = jnp.broadcast_to(held[None], (8,) + held.shape)
    mine = lax.all_to_all(sent, "panel", 0, 0, axis_index_groups=groups)
    theirs = lax.ppermute(mine, AXES, pairs(to_core))
    half = update(update_own_kernel, "update_own", (scaled, sibling, mine), sep_stiffness, None)
    return update(update_other_kernel, "update_other", (scaled, sibling, mine, theirs), sep_stiffness, half)


def solution(mesh):
    placed = (
        P("leaf", "panel", None),
        P("leaf", None, None),
        P("leaf", None),
        P("leaf", "panel", None),
    )
    return jax.shard_map(
        shards, mesh=mesh, in_specs=placed, out_specs=P("leaf", "panel", None), check_vma=False
    )
```

```python
import functools

import jax
import jax.numpy as jnp
from jax import lax
from jax.experimental import pallas as pl
from jax.experimental.pallas import tpu as pltpu
from jax.sharding import PartitionSpec as P

AXES = ("leaf", "panel")
PANELS = 16
PROJECT_VMEM = 211 * 2**18
VMEM = pl.BlockSpec(memory_space=pltpu.VMEM)
HBM = pl.BlockSpec(memory_space=pltpu.HBM)


def pairs(move):
    found = []
    for parent in range(lax.axis_size("leaf") // 2):
        for bit in range(2):
            for panel in range(PANELS):
                target = move(bit, panel)
                if target is not None:
                    found.append((
                        (2 * parent + bit) * PANELS + panel,
                        (2 * parent + target[0]) * PANELS + target[1],
                    ))
    return found


def across(bit, panel):
    return None if panel // 8 == bit else (1 - bit, panel ^ 14)


def to_sibling(bit, panel):
    return (1 - bit, panel) if panel // 8 == bit else None


def to_core(bit, panel):
    return (bit, panel ^ 1)


def project_kernel(parts, coupling, modes, projected, a, b, sems):
    depth = a.shape[1] // parts
    copies = []
    for k in range(parts):
        cut = pl.ds(k * depth, depth)
        copies.append((
            pltpu.make_async_copy(coupling.at[0, :, cut], a.at[:, cut], sems.at[0, k]),
            pltpu.make_async_copy(modes.at[0, cut, :], b.at[cut, :], sems.at[1, k]),
        ))
    for pair in copies:
        for copy in pair:
            copy.start()
    total = None
    for k, pair in enumerate(copies):
        for copy in pair:
            copy.wait()
        term = jnp.dot(
            a[:, k * depth : (k + 1) * depth],
            b[k * depth : (k + 1) * depth, :],
            preferred_element_type=jnp.float32,
        )
        total = term if total is None else total + term
    projected[...] = total


def project(coupling, modes):
    rows, depth, columns = coupling.shape[1], coupling.shape[2], modes.shape[2]
    parts = 2
    return pl.pallas_call(
        functools.partial(project_kernel, parts),
        out_shape=jax.ShapeDtypeStruct((rows, columns), jnp.float32),
        in_specs=[HBM, HBM],
        out_specs=VMEM,
        scratch_shapes=[
            pltpu.VMEM((rows, depth), jnp.bfloat16),
            pltpu.VMEM((depth, columns), jnp.bfloat16),
            pltpu.SemaphoreType.DMA((2, parts)),
        ],
        compiler_params=pltpu.CompilerParams(vmem_limit_bytes=PROJECT_VMEM),
        name="project",
    )(coupling, modes)


def update_kernel(other_core, own, sibling, mine, pieces, stiffness, out, made, sems):
    bit, panel = lax.axis_index("leaf") % 2, lax.axis_index("panel")
    core = 1 - panel % 2 if other_core else panel % 2
    here = panel // 8 == bit
    width = own.shape[0]
    partner = jnp.where(here, mine[(1 - bit) * 4 + 3 - (panel % 8) // 2], sibling[...])
    stores = []
    for n in range(4):
        cut = pl.ds(pl.multiple_of((2 * n + core) * width, width), width)
        block = lax.dot_general(
            own[...], pieces[bit * 4 + n], (((1,), (1,)), ((), ())), preferred_element_type=jnp.float32
        ) + lax.dot_general(
            partner,
            pieces[(1 - bit) * 4 + 3 - n],
            (((1,), (1,)), ((), ())),
            preferred_element_type=jnp.float32,
        )
        made[n] = (stiffness[0, :, cut].astype(jnp.float32) - block).astype(jnp.bfloat16)
        stores.append(pltpu.make_async_copy(made.at[n], out.at[0, :, cut], sems.at[n]))
        stores[n].start()
    for copy in stores:
        copy.wait()


def update_own_kernel(own, sibling, mine, stiffness, *rest):
    update_kernel(False, own, sibling, mine, mine, stiffness, *rest)


def update_other_kernel(own, sibling, mine, theirs, stiffness, so_far, *rest):
    del so_far
    update_kernel(True, own, sibling, mine, theirs, stiffness, *rest)


def update(kernel, name, arrays, stiffness, so_far):
    rows = arrays[0].shape[0]
    before = [] if so_far is None else [so_far]
    count = len(arrays) + 1
    return pl.pallas_call(
        kernel,
        out_shape=jax.ShapeDtypeStruct(stiffness.shape, stiffness.dtype),
        in_specs=[VMEM] * count + [HBM] * len(before),
        out_specs=HBM,
        scratch_shapes=[
            pltpu.VMEM((4, rows, rows), jnp.bfloat16),
            pltpu.SemaphoreType.DMA((4,)),
        ],
        input_output_aliases={count: 0} if before else {},
        compiler_params=pltpu.CompilerParams(vmem_limit_bytes=16 * 2**20),
        cost_estimate=pl.CostEstimate(
            flops=10**8 if before else 10**10, bytes_accessed=2 * 2**20, transcendentals=0
        ),
        name=name,
    )(*arrays, stiffness, *before)


def shards(coupling, modes, eigvals, sep_stiffness):
    projected, eigvals = lax.optimization_barrier((project(coupling, modes), eigvals))
    scaled = (projected * lax.rsqrt(eigvals[0])[None, :]).astype(jnp.bfloat16)
    bit = lax.axis_index("leaf") % 2
    here = lax.axis_index("panel") // 8 == bit

    sibling = lax.ppermute(scaled, AXES, pairs(to_sibling))
    crossed = lax.ppermute(scaled, AXES, pairs(across))
    held = jnp.where(here, scaled, crossed)
    groups = [list(range(core, PANELS, 2)) for core in range(2)]
    sent = jnp.broadcast_to(held[None], (8,) + held.shape)
    mine = lax.cond(
        lax.axis_index("panel") < PANELS,
        lambda x: lax.all_to_all(x, "panel", 0, 0, axis_index_groups=groups),
        lambda x: x,
        sent,
    )
    theirs = lax.ppermute(mine, AXES, pairs(to_core))
    half = update(update_own_kernel, "update_own", (scaled, sibling, mine), sep_stiffness, None)
    return update(update_other_kernel, "update_other", (scaled, sibling, mine, theirs), sep_stiffness, half)


def solution(mesh):
    placed = (
        P("leaf", "panel", None),
        P("leaf", None, None),
        P("leaf", None),
        P("leaf", "panel", None),
    )
    return jax.shard_map(
        shards, mesh=mesh, in_specs=placed, out_specs=P("leaf", "panel", None), check_vma=False
    )
```

```python
import functools

import jax
import jax.numpy as jnp
from jax import lax
from jax.experimental import pallas as pl
from jax.experimental.pallas import tpu as pltpu
from jax.sharding import PartitionSpec as P

AXES = ("leaf", "panel")
PANELS = 16
PROJECT_VMEM = 211 * 2**18
VMEM = pl.BlockSpec(memory_space=pltpu.VMEM)
HBM = pl.BlockSpec(memory_space=pltpu.HBM)


def pairs(move):
    found = []
    for parent in range(lax.axis_size("leaf") // 2):
        for bit in range(2):
            for panel in range(PANELS):
                target = move(bit, panel)
                if target is not None:
                    found.append((
                        (2 * parent + bit) * PANELS + panel,
                        (2 * parent + target[0]) * PANELS + target[1],
                    ))
    return found


def shift(bit, panel):
    if panel // 8 == bit:
        return (bit, panel ^ 12) if (bit, panel) != (0, 0) else None
    return (1 - bit, panel ^ 2) if (bit, panel) != (1, 2) else (0, 12)


def own_at(bit, core, n):
    usual = (1 - bit) * 4 + (n ^ 2)
    return jnp.where((bit == 0) & (core == 0), 0, usual) if n == 0 else usual


def other_at(bit, core, n):
    usual = bit * 4 + (n ^ 1)
    return jnp.where((bit == 0) & (core == 0) & (n == 1), 6, usual)


def to_sibling(bit, panel):
    return (1 - bit, panel) if panel // 8 == bit else None


def to_core(bit, panel):
    return (bit, panel ^ 1)


def project_kernel(parts, coupling, modes, projected, a, b, sems):
    depth = a.shape[1] // parts
    copies = []
    for k in range(parts):
        cut = pl.ds(k * depth, depth)
        copies.append((
            pltpu.make_async_copy(coupling.at[0, :, cut], a.at[:, cut], sems.at[0, k]),
            pltpu.make_async_copy(modes.at[0, cut, :], b.at[cut, :], sems.at[1, k]),
        ))
    for pair in copies:
        for copy in pair:
            copy.start()
    total = None
    for k, pair in enumerate(copies):
        for copy in pair:
            copy.wait()
        term = jnp.dot(
            a[:, k * depth : (k + 1) * depth],
            b[k * depth : (k + 1) * depth, :],
            preferred_element_type=jnp.float32,
        )
        total = term if total is None else total + term
    projected[...] = total


def project(coupling, modes):
    rows, depth, columns = coupling.shape[1], coupling.shape[2], modes.shape[2]
    parts = 2
    return pl.pallas_call(
        functools.partial(project_kernel, parts),
        out_shape=jax.ShapeDtypeStruct((rows, columns), jnp.float32),
        in_specs=[HBM, HBM],
        out_specs=VMEM,
        scratch_shapes=[
            pltpu.VMEM((rows, depth), jnp.bfloat16),
            pltpu.VMEM((depth, columns), jnp.bfloat16),
            pltpu.SemaphoreType.DMA((2, parts)),
        ],
        compiler_params=pltpu.CompilerParams(vmem_limit_bytes=PROJECT_VMEM),
        name="project",
    )(coupling, modes)


def update_kernel(other_core, own, sibling, mine, pieces, stiffness, out, made, sems):
    bit, panel = lax.axis_index("leaf") % 2, lax.axis_index("panel")
    core = 1 - panel % 2 if other_core else panel % 2
    here = panel // 8 == bit
    width = own.shape[0]
    place = panel % 8 // 2
    partner = mine[other_at(bit, panel % 2, place)]
    partner = jnp.where(here, partner, sibling[...])
    stores = []
    for n in range(4):
        cut = pl.ds(pl.multiple_of((2 * n + core) * width, width), width)
        block = lax.dot_general(
            own[...], pieces[own_at(bit, core, n)], (((1,), (1,)), ((), ())), preferred_element_type=jnp.float32
        ) + lax.dot_general(
            partner,
            pieces[other_at(bit, core, n)],
            (((1,), (1,)), ((), ())),
            preferred_element_type=jnp.float32,
        )
        made[n] = (stiffness[0, :, cut].astype(jnp.float32) - block).astype(jnp.bfloat16)
        stores.append(pltpu.make_async_copy(made.at[n], out.at[0, :, cut], sems.at[n]))
        stores[n].start()
    for copy in stores:
        copy.wait()


def update_own_kernel(own, sibling, mine, stiffness, *rest):
    update_kernel(False, own, sibling, mine, mine, stiffness, *rest)


def update_other_kernel(own, sibling, mine, theirs, stiffness, so_far, *rest):
    del so_far
    update_kernel(True, own, sibling, mine, theirs, stiffness, *rest)


def update(kernel, name, arrays, stiffness, so_far):
    rows = arrays[0].shape[0]
    before = [] if so_far is None else [so_far]
    count = len(arrays) + 1
    return pl.pallas_call(
        kernel,
        out_shape=jax.ShapeDtypeStruct(stiffness.shape, stiffness.dtype),
        in_specs=[VMEM] * count + [HBM] * len(before),
        out_specs=HBM,
        scratch_shapes=[
            pltpu.VMEM((4, rows, rows), jnp.bfloat16),
            pltpu.SemaphoreType.DMA((4,)),
        ],
        input_output_aliases={count: 0} if before else {},
        compiler_params=pltpu.CompilerParams(vmem_limit_bytes=16 * 2**20),
        cost_estimate=pl.CostEstimate(
            flops=10**8 if before else 10**10, bytes_accessed=2 * 2**20, transcendentals=0
        ),
        name=name,
    )(*arrays, stiffness, *before)


def spread(piece):
    return jnp.broadcast_to(piece[None], (8,) + piece.shape)


def shards(coupling, modes, eigvals, sep_stiffness):
    projected, eigvals = lax.optimization_barrier((project(coupling, modes), eigvals))
    scaled = (projected * lax.rsqrt(eigvals[0])[None, :]).astype(jnp.bfloat16)
    bit, panel = lax.axis_index("leaf") % 2, lax.axis_index("panel")
    sibling = lax.ppermute(scaled, AXES, pairs(to_sibling))
    moved = lax.ppermute(scaled, AXES, pairs(shift))
    keeps = (bit == 0) & (panel == 0)
    held = jnp.where(keeps, scaled, moved)
    groups = [list(range(core, PANELS, 2)) for core in range(2)]
    mine = lax.cond(
        lax.axis_index("panel") < PANELS,
        lambda x: lax.all_to_all(spread(x), "panel", 0, 0, axis_index_groups=groups),
        spread,
        held,
    )
    theirs = lax.ppermute(mine, AXES, pairs(to_core))
    half = update(update_own_kernel, "update_own", (scaled, sibling, mine), sep_stiffness, None)
    return update(update_other_kernel, "update_other", (scaled, sibling, mine, theirs), sep_stiffness, half)


def solution(mesh):
    placed = (
        P("leaf", "panel", None),
        P("leaf", None, None),
        P("leaf", None),
        P("leaf", "panel", None),
    )
    return jax.shard_map(
        shards, mesh=mesh, in_specs=placed, out_specs=P("leaf", "panel", None), check_vma=False
    )
```

```python
import functools

import jax
import jax.numpy as jnp
from jax import lax
from jax.experimental import pallas as pl
from jax.experimental.pallas import tpu as pltpu
from jax.sharding import PartitionSpec as P

AXES = ("leaf", "panel")
PANELS = 16
PROJECT_VMEM = 211 * 2**18
VMEM = pl.BlockSpec(memory_space=pltpu.VMEM)
HBM = pl.BlockSpec(memory_space=pltpu.HBM)


def pairs(move):
    found = []
    for parent in range(lax.axis_size("leaf") // 2):
        for bit in range(2):
            for panel in range(PANELS):
                target = move(parent, bit, panel)
                if target is not None:
                    found.append((
                        (2 * parent + bit) * PANELS + panel,
                        (2 * parent + target[0]) * PANELS + target[1],
                    ))
    return found


def shift(parent, bit, panel):
    if panel // 8 == bit:
        return (bit, panel ^ 12) if (parent, bit, panel) != (0, 0, 0) else None
    return (1 - bit, panel ^ 2) if (parent, bit, panel) != (0, 1, 2) else (0, 12)


def own_at(leaf, core, n):
    usual = (1 - leaf % 2) * 4 + (n ^ 2)
    return jnp.where((leaf == 0) & (core == 0), 0, usual) if n == 0 else usual


def other_at(leaf, core, n):
    usual = leaf % 2 * 4 + (n ^ 1)
    return jnp.where((leaf == 0) & (core == 0) & (n == 1), 6, usual)


def to_sibling(parent, bit, panel):
    return (1 - bit, panel) if panel // 8 == bit else None


def to_core(parent, bit, panel):
    return (bit, panel ^ 1)


def project_kernel(parts, coupling, modes, projected, a, b, sems):
    depth = a.shape[1] // parts
    copies = []
    for k in range(parts):
        cut = pl.ds(k * depth, depth)
        copies.append((
            pltpu.make_async_copy(coupling.at[0, :, cut], a.at[:, cut], sems.at[0, k]),
            pltpu.make_async_copy(modes.at[0, cut, :], b.at[cut, :], sems.at[1, k]),
        ))
    for pair in copies:
        for copy in pair:
            copy.start()
    total = None
    for k, pair in enumerate(copies):
        for copy in pair:
            copy.wait()
        term = jnp.dot(
            a[:, k * depth : (k + 1) * depth],
            b[k * depth : (k + 1) * depth, :],
            preferred_element_type=jnp.float32,
        )
        total = term if total is None else total + term
    projected[...] = total


def project(coupling, modes):
    rows, depth, columns = coupling.shape[1], coupling.shape[2], modes.shape[2]
    parts = 2
    return pl.pallas_call(
        functools.partial(project_kernel, parts),
        out_shape=jax.ShapeDtypeStruct((rows, columns), jnp.float32),
        in_specs=[HBM, HBM],
        out_specs=VMEM,
        scratch_shapes=[
            pltpu.VMEM((rows, depth), jnp.bfloat16),
            pltpu.VMEM((depth, columns), jnp.bfloat16),
            pltpu.SemaphoreType.DMA((2, parts)),
        ],
        compiler_params=pltpu.CompilerParams(vmem_limit_bytes=PROJECT_VMEM),
        name="project",
    )(coupling, modes)


def update_kernel(other_core, own, sibling, mine, pieces, stiffness, out, made, sems):
    leaf, panel = lax.axis_index("leaf"), lax.axis_index("panel")
    core = 1 - panel % 2 if other_core else panel % 2
    here = panel // 8 == leaf % 2
    width = own.shape[0]
    place = panel % 8 // 2
    partner = mine[other_at(leaf, panel % 2, place)]
    partner = jnp.where(here, partner, sibling[...])
    stores = []
    for n in range(4):
        cut = pl.ds(pl.multiple_of((2 * n + core) * width, width), width)
        block = lax.dot_general(
            own[...], pieces[own_at(leaf, core, n)], (((1,), (1,)), ((), ())), preferred_element_type=jnp.float32
        ) + lax.dot_general(
            partner,
            pieces[other_at(leaf, core, n)],
            (((1,), (1,)), ((), ())),
            preferred_element_type=jnp.float32,
        )
        made[n] = (stiffness[0, :, cut].astype(jnp.float32) - block).astype(jnp.bfloat16)
        stores.append(pltpu.make_async_copy(made.at[n], out.at[0, :, cut], sems.at[n]))
        stores[n].start()
    for copy in stores:
        copy.wait()


def update_own_kernel(own, sibling, mine, stiffness, *rest):
    update_kernel(False, own, sibling, mine, mine, stiffness, *rest)


def update_other_kernel(own, sibling, mine, theirs, stiffness, so_far, *rest):
    del so_far
    update_kernel(True, own, sibling, mine, theirs, stiffness, *rest)


def update(kernel, name, arrays, stiffness, so_far):
    rows = arrays[0].shape[0]
    before = [] if so_far is None else [so_far]
    count = len(arrays) + 1
    return pl.pallas_call(
        kernel,
        out_shape=jax.ShapeDtypeStruct(stiffness.shape, stiffness.dtype),
        in_specs=[VMEM] * count + [HBM] * len(before),
        out_specs=HBM,
        scratch_shapes=[
            pltpu.VMEM((4, rows, rows), jnp.bfloat16),
            pltpu.SemaphoreType.DMA((4,)),
        ],
        input_output_aliases={count: 0} if before else {},
        compiler_params=pltpu.CompilerParams(vmem_limit_bytes=16 * 2**20),
        cost_estimate=pl.CostEstimate(
            flops=10**8 if before else 10**10, bytes_accessed=2 * 2**20, transcendentals=0
        ),
        name=name,
    )(*arrays, stiffness, *before)


def spread(piece):
    return jnp.broadcast_to(piece[None], (8,) + piece.shape)


def shards(coupling, modes, eigvals, sep_stiffness):
    projected, eigvals = lax.optimization_barrier((project(coupling, modes), eigvals))
    scaled = (projected * lax.rsqrt(eigvals[0])[None, :]).astype(jnp.bfloat16)
    leaf, panel = lax.axis_index("leaf"), lax.axis_index("panel")
    sibling = lax.ppermute(scaled, AXES, pairs(to_sibling))
    moved = lax.ppermute(scaled, AXES, pairs(shift))
    keeps = (leaf == 0) & (panel == 0)
    held = jnp.where(keeps, scaled, moved)
    groups = [list(range(core, PANELS, 2)) for core in range(2)]
    mine = lax.cond(
        lax.axis_index("panel") < PANELS,
        lambda x: lax.all_to_all(spread(x), "panel", 0, 0, axis_index_groups=groups),
        spread,
        held,
    )
    theirs = lax.ppermute(mine, AXES, pairs(to_core))
    half = update(update_own_kernel, "update_own", (scaled, sibling, mine), sep_stiffness, None)
    return update(update_other_kernel, "update_other", (scaled, sibling, mine, theirs), sep_stiffness, half)


def solution(mesh):
    placed = (
        P("leaf", "panel", None),
        P("leaf", None, None),
        P("leaf", None),
        P("leaf", "panel", None),
    )
    return jax.shard_map(
        shards, mesh=mesh, in_specs=placed, out_specs=P("leaf", "panel", None), check_vma=False
    )
```
